512 devices in a mesh: replica: 4 (over z_hi, core), fsdp: 32 (over x, z_lo), tensor: 4 (over y).
Axes of the slice: x: 4, y: 4, z: 16 (z_hi: 2, z_lo: 8; z = z_hi * 8 + z_lo), core: 2. Of those that a mesh axis runs over, the one named last changes fastest.
Arguments:
- tokens: bfloat16 [65536, 8192], P(('replica', 'fsdp', 'tensor')), may hold values from -6 to 6
- cotangent: bfloat16 [65536, 2, 512], P(('replica', 'fsdp'), None, 'tensor'), may hold values from -0.125 to 0.125
- weights: bfloat16 [4, 8192, 2, 512], P('replica', 'fsdp', None, 'tensor'), may hold values from -0.0625 to 0.0625
- first_moment: float32 [4, 8192, 2, 512], P('replica', 'fsdp', None, 'tensor'), may hold values from -6 to 6
- second_moment: float32 [4, 8192, 2, 512], P('replica', 'fsdp', None, 'tensor'), may hold values from 0.5 to 2
- frag_global: float32 [8192, 2, 512], P('fsdp', None, 'tensor'), may hold values from -6 to 6
- frag_moment: float32 [8192, 2, 512], P('fsdp', None, 'tensor'), may hold values from -6 to 6
- frag_local: bfloat16 [4, 8192, 2, 512], P('replica', 'fsdp', None, 'tensor'), may hold values from -6 to 6
Outputs:
- keys_values: bfloat16 [65536, 2, 512], P(('replica', 'fsdp'), None, 'tensor')
- weights_next: bfloat16 [4, 8192, 2, 512], P('replica', 'fsdp', None, 'tensor')
- first_next: float32 [4, 8192, 2, 512], P('replica', 'fsdp', None, 'tensor')
- second_next: float32 [4, 8192, 2, 512], P('replica', 'fsdp', None, 'tensor')
- global_next: float32 [8192, 2, 512], P('fsdp', None, 'tensor')
- moment_next: float32 [8192, 2, 512], P('fsdp', None, 'tensor')
- local_next: bfloat16 [4, 8192, 2, 512], P('replica', 'fsdp', None, 'tensor')
The draws below stay inside these ranges and needn't reach their ends.
All inputs are finite; a program needn't handle non-finite values.
Results may differ from the reference program's by a relative error of at most 0.009.
Values may be sent and summed in bfloat16 or wider, within the bound.
No kernel may reach another device: no remote copies, remote signals or barrier semaphores. Data moves between devices by JAX's collectives and lax.ppermute only.
A program may use at most 128 MiB of HBM per device.

```python
import math
import jax
import jax.numpy as jnp
from jax import lax

D = 8192
HD = 128
KVH = 4
TOK_DEV = 512
KVW = 512
REPLICAS = 4
TOKENS = 65536
N_REPLICA = 4
N_FSDP = 32


def block_scale(stream_key, extent, cuts, smallest, high):
    gain = 1.0
    for position, shards_of in cuts:
        heights = jax.random.uniform(jax.random.fold_in(jax.random.fold_in(stream_key, 6), position), (shards_of,), jnp.float32, smallest / len(cuts), high / len(cuts))
        gain = gain * jnp.repeat(jnp.exp(heights), extent[position] // shards_of).reshape((-1,) + (1,) * (len(extent) - 1 - position))
    return gain


def normal_values(own_key, extent, scale, most, shards=(), kind=jnp.bfloat16):
    factor_of = block_scale(own_key, extent, shards, -0.22, 0.18) if shards else 1.0
    drawn = jax.random.normal(own_key, extent, jnp.float32) * scale * factor_of
    return jnp.minimum(jnp.maximum(drawn, -most), most).astype(kind)


def setup_inputs(seed: int = 0) -> dict:
    key_of = jax.random.split(jax.random.key(seed), 9)
    return {
        "tokens": normal_values(key_of[0], (TOKENS, D), 1.0, 6.0, ((0, 512),)),
        "cotangent": normal_values(key_of[1], (TOKENS, 2, KVW), ((TOK_DEV * N_FSDP) ** -0.5), 0.125, ((0, 128), (2, 4))),
        "weights": normal_values(key_of[2], (REPLICAS, D, 2, KVW), D ** -0.5, 0.0625, ((0, 4), (1, 32), (3, 4))),
        "first_moment": normal_values(key_of[3], (REPLICAS, D, 2, KVW), 1.0, 6.0, ((0, 4), (1, 32), (3, 4)), jnp.float32),
        "second_moment": jnp.clip(jnp.exp(math.log(2.0) - 1.3862944 * jax.random.uniform(key_of[4], (REPLICAS, D, 2, KVW), jnp.float32) ** block_scale(key_of[4], (REPLICAS, D, 2, KVW), ((0, 4), (1, 32), (3, 4)), -0.2, 0.2)), 0.5, 2.0),
        "frag_global": normal_values(key_of[5], (D, 2, KVW), 1.0, 6.0, ((0, 32), (2, 4)), jnp.float32),
        "frag_moment": normal_values(key_of[6], (D, 2, KVW), 0.5, 6.0, ((0, 32), (2, 4)), jnp.float32),
        "frag_local": normal_values(key_of[7], (REPLICAS, D, 2, KVW), 1.0, 6.0, ((0, 4), (1, 32), (3, 4))),
    }


def reference(tokens, cotangent, weights, first_moment, second_moment, frag_global, frag_moment, frag_local):
    kv_width = 2 * KVH * HD
    block_rows = N_FSDP * TOK_DEV
    projected = []
    gradients = []
    for replica_index in range(N_REPLICA):
        token_block = tokens[replica_index * block_rows:(replica_index + 1) * block_rows]
        cot_block = cotangent[replica_index * block_rows:(replica_index + 1) * block_rows].reshape(block_rows, kv_width)
        flat_weight = weights[replica_index].reshape(D, kv_width)
        projected.append(jnp.dot(token_block, flat_weight, preferred_element_type=jnp.float32).astype(jnp.bfloat16))
        token_parts = token_block.reshape(N_FSDP, TOK_DEV, D)
        cot_parts = cot_block.reshape(N_FSDP, TOK_DEV, kv_width)

        def add_part(running, operands):
            left_part, right_part = operands
            partial_term = jnp.dot(left_part.T, right_part, preferred_element_type=jnp.float32).astype(jnp.bfloat16)
            partial_term = lax.optimization_barrier(partial_term)
            return (running + partial_term.astype(jnp.float32), None)
        summed, unused = lax.scan(add_part, jnp.zeros((D, kv_width), jnp.float32), (token_parts, cot_parts))
        gradients.append(summed.reshape(D, 2, KVH * HD))
    keys_values = jnp.concatenate(projected, axis=0).reshape(-1, 2, KVH * HD)
    gradient = jnp.stack(gradients)
    first_next = 0.9 * first_moment + 0.1 * gradient
    second_next = 0.95 * second_moment + 0.05 * gradient * gradient
    weight_float = weights.astype(jnp.float32)
    update = first_next / (1.0 - 0.9 ** 10) / (jnp.sqrt(second_next / (1.0 - 0.95 ** 10)) + 1e-08)
    weights_next = (weight_float - 0.001 * (update + 0.1 * weight_float)).astype(jnp.bfloat16)
    local_sum = lax.optimization_barrier(jnp.sum(frag_local.astype(jnp.float32), axis=0))
    outer_step = frag_global - local_sum / N_REPLICA
    moment_next = 0.9 * frag_moment + outer_step
    global_next = frag_global - 0.7 * (outer_step + 0.9 * moment_next)
    local_next = (0.5 * frag_local.astype(jnp.float32) + 0.5 * global_next[None]).astype(jnp.bfloat16)
    return (keys_values, weights_next, first_next, second_next, global_next, moment_next, local_next)
```

```python
import jax
import jax.numpy as jnp
from jax import lax
from jax.sharding import PartitionSpec as P

NX, NZ, NY = 4, 8, 4


def move_x(value, shift):
    pairs = [(NZ * x + z, NZ * ((x + shift) % NX) + z) for x in range(NX) for z in range(NZ)]
    return lax.ppermute(value, "fsdp", pairs)


def move_z(value, shift):
    pairs = [(NZ * x + z, NZ * x + (z + shift) % NZ) for x in range(NX) for z in range(NZ)]
    return lax.ppermute(value, "fsdp", pairs)


def move_y(value, shift):
    return lax.ppermute(value, "tensor", [(y, (y + shift) % NY) for y in range(NY)])


def body(
    tokens, cotangent, weights, first_moment, second_moment, frag_global, frag_moment, frag_local
):
    rows, width = tokens.shape
    depth = weights.shape[1]
    columns = weights.shape[2] * weights.shape[3]
    chunk = width // NX
    x = lax.axis_index("fsdp") // NZ
    z = lax.axis_index("fsdp") % NZ
    y = lax.axis_index("tensor")

    local_float = frag_local[0].astype(jnp.float32)
    summed = lax.psum(frag_local[0], "replica").astype(jnp.float32)
    outer_step = frag_global - summed / lax.axis_size("replica")
    moment_next = 0.9 * frag_moment + outer_step
    global_next = frag_global - 0.7 * (outer_step + 0.9 * moment_next)
    local_next = (0.5 * local_float + 0.5 * global_next).astype(jnp.bfloat16)[None]

    def gather_rows(j):
        own = lax.dynamic_slice_in_dim(tokens, (x + j) % NX * chunk, chunk, axis=1)
        before = move_y(own, 1)
        after = move_y(own, -1)
        first = move_y(before[: rows // 2], 1)
        second = move_y(after[rows // 2 :], -1)
        return jnp.concatenate([own, before, after, first, second], axis=0)

    held = {j: gather_rows(j) for j in (2, 1, 3, 0)}
    order = jnp.stack([y, (y + 3) % NY, (y + 1) % NY, (y + 2) % NY])
    cot = cotangent.reshape(NY, rows, columns)[order].reshape(NY * rows, columns)

    own = weights[0].reshape(depth, columns)
    blocks = [own] + [move_z(own, -s) for s in range(1, NZ)]
    blocks = jnp.concatenate(blocks + blocks, axis=0)
    plane = lax.dynamic_slice_in_dim(blocks, (NZ - z) * depth, NZ * depth, axis=0)
    plane_before = move_x(plane, 1)
    plane_after = move_x(plane, -1)
    half = NZ * depth // 2
    plane_far = jnp.concatenate(
        [move_x(plane_before[:half], 1), move_x(plane_after[half:], -1)], axis=0
    )
    planes = {0: plane, 1: plane_after, 2: plane_far, 3: plane_before}

    def term(j):
        return lax.dot_general(
            held[j], cot, (((0,), (0,)), ((), ())), preferred_element_type=jnp.float32
        ).astype(jnp.bfloat16)

    far = term(2)
    far_first = move_x(far[:half], 1)
    far_second = move_x(far[half:], -1)
    up = term(1)
    up = jnp.concatenate([up[:half] + far_first, up[half:]], axis=0)
    from_before = move_x(up, 1)
    down = term(3)
    down = jnp.concatenate([down[:half], down[half:] + far_second], axis=0)
    from_after = move_x(down, -1)
    mine = term(0).astype(jnp.float32)
    mine = mine + from_before.astype(jnp.float32) + from_after.astype(jnp.float32)
    sent = mine.astype(jnp.bfloat16)
    gradient = lax.dynamic_slice_in_dim(mine, z * depth, depth, axis=0)
    for s in range(1, NZ):
        block = lax.dynamic_slice_in_dim(sent, (z + s) % NZ * depth, depth, axis=0)
        gradient = gradient + move_z(block, s).astype(jnp.float32)

    projected = sum(
        jnp.dot(held[j], planes[j], preferred_element_type=jnp.float32) for j in (2, 1, 3, 0)
    )
    back = jnp.stack([(p - y) % NY for p in range(NY)])
    place = jnp.array([0, 2, 3, 1])[back]
    keys_values = projected.astype(jnp.bfloat16).reshape(NY, rows, columns)[place]
    keys_values = keys_values.reshape(cotangent.shape)

    gradient = gradient.reshape(first_moment.shape)
    first_next = 0.9 * first_moment + 0.1 * gradient
    second_next = 0.95 * second_moment + 0.05 * gradient * gradient
    weight_float = weights.astype(jnp.float32)
    update = first_next / (1.0 - 0.9**10) / (jnp.sqrt(second_next / (1.0 - 0.95**10)) + 1e-08)
    weights_next = (weight_float - 0.001 * (update + 0.1 * weight_float)).astype(jnp.bfloat16)
    return (
        keys_values,
        weights_next,
        first_next,
        second_next,
        global_next,
        moment_next,
        local_next,
    )


def solution(mesh):
    return jax.shard_map(
        body,
        mesh=mesh,
        in_specs=(
            P(("replica", "fsdp", "tensor"), None),
            P(("replica", "fsdp"), None, "tensor"),
            P("replica", "fsdp", None, "tensor"),
            P("replica", "fsdp", None, "tensor"),
            P("replica", "fsdp", None, "tensor"),
            P("fsdp", None, "tensor"),
            P("fsdp", None, "tensor"),
            P("replica", "fsdp", None, "tensor"),
        ),
        out_specs=(
            P(("replica", "fsdp"), None, "tensor"),
            P("replica", "fsdp", None, "tensor"),
            P("replica", "fsdp", None, "tensor"),
            P("replica", "fsdp", None, "tensor"),
            P("fsdp", None, "tensor"),
            P("fsdp", None, "tensor"),
            P("replica", "fsdp", None, "tensor"),
        ),
        check_vma=False,
    )
```

```python
import jax
import jax.numpy as jnp
from jax import lax
from jax.sharding import PartitionSpec as P

NX, NZ, NY = 4, 8, 4
HALF = NZ // 2
BF16, F32 = jnp.bfloat16, jnp.float32


def move(value, target):
    pairs = []
    for x in range(NX):
        for z in range(NZ):
            to_x, to_z = target(x, z)
            pairs.append((NZ * x + z, NZ * (to_x % NX) + to_z))
    return lax.ppermute(value, "fsdp", pairs)


def move_x(value, shift):
    return move(value, lambda x, z: (x + shift, z))


def move_y(value, shift):
    return lax.ppermute(value, "tensor", [(y, (y + shift) % NY) for y in range(NY)])


def swap_z(value, bit):
    return move(value, lambda x, z: (x, z ^ bit))


def swap_replica(value, bit):
    return lax.ppermute(value, "replica", [(r, r ^ bit) for r in range(lax.axis_size("replica"))])


def after(value, *others):
    return lax.optimization_barrier((value, *others))[0]


def body(
    tokens, cotangent, weights, first_moment, second_moment, frag_global, frag_moment, frag_local
):
    rows, width = tokens.shape
    depth = weights.shape[1]
    columns = weights.shape[2] * weights.shape[3]
    part = HALF * depth
    x = lax.axis_index("fsdp") // NZ
    z = lax.axis_index("fsdp") % NZ
    side = z // HALF
    y = lax.axis_index("tensor")

    def chunk(j, other):
        start = (x + j) % NX * (NZ * depth) + (side ^ other) * part
        return lax.dynamic_slice_in_dim(tokens, start, part, axis=1)

    held = []
    ready = ()
    for other in (1, 0):
        sent = jnp.concatenate([chunk(j, other) for j in (2, 1, 3, 0)], axis=1)
        sent = after(sent, *ready)
        before, behind = move_y(sent, 1), move_y(sent, -1)
        front, back = lax.optimization_barrier((before[: rows // 2], behind[rows // 2 :]))
        if other:
            arrived = front
        first, second = move_y(front, 1), move_y(back, -1)
        rest = jnp.concatenate([sent, before, behind], axis=0)
        rest = lax.optimization_barrier(jnp.pad(rest, ((0, rows), (0, 0))))
        ready = (rest,)
        rest = lax.dynamic_update_slice(rest, first, (3 * rows, 0))
        held.append(lax.dynamic_update_slice(rest, second, (3 * rows + rows // 2, 0)))
    far_held, near_held = held
    cot = cotangent.reshape(NY, rows, columns)
    cot = jnp.concatenate(
        [lax.dynamic_slice_in_dim(cot, (y + k) % NY, 1, axis=0) for k in (0, 3, 1, 2)], axis=0
    ).reshape(NY * rows, columns)

    own = weights[0].reshape(1, depth, columns)
    two = jnp.stack([own, swap_z(own, 4)])
    four = jnp.stack([two, swap_z(two, 2)])
    four = after(four, arrived)
    eight = jnp.stack([four, swap_z(four, 1)])
    eight = eight.reshape(2, 2, 2, depth, columns)
    eight = jnp.where((z & 1) == 0, eight, eight[::-1])
    eight = jnp.where((z & 2) == 0, eight, eight[:, ::-1])
    eight = jnp.where((z & 4) == 0, eight, eight[:, :, ::-1])
    plane = eight.transpose(2, 1, 0, 3, 4).reshape(2 * part, columns)
    def terms(held):
        product = lax.dot_general(held, cot, (((0,), (0,)), ((), ())), preferred_element_type=F32)
        return product.astype(BF16).reshape(NX, part, columns)

    def send_x(opposite, up, down, sign):
        if sign < 0:
            up, down = down, up
        passed = move_x(opposite, sign)
        reverse = move_x(down, -sign)
        return (up.astype(F32) + passed.astype(F32)).astype(BF16), reverse

    def block(value, index, count=1):
        return lax.dynamic_slice_in_dim(value, index * depth, count * depth, axis=0)

    opposite, up, down, here = terms(far_held)
    up, reverse = send_x(opposite, up, down, 1)
    forward = move_x(up, 1)
    far = here.astype(F32) + reverse.astype(F32) + forward.astype(F32)
    far = far.astype(BF16)
    crossing = swap_z(far, 4)

    plane = after(plane, far)
    low = move_x(plane, 1)
    high = move_x(plane, -1)
    planes = {0: plane, 1: high, 2: move_x(low, 1), 3: low}

    opposite, up, down, here = terms(near_held)
    down, reverse = send_x(opposite, up, down, -1)
    forward = move_x(down, -1)
    near = here.astype(F32) + reverse.astype(F32) + forward.astype(F32) + crossing.astype(F32)
    sent = near.astype(BF16)
    quarter = z % HALF
    pieces = [swap_z(block(sent, quarter ^ k), k) for k in range(1, HALF)]
    def half_plane(j, other):
        return lax.dynamic_slice_in_dim(planes[j], (side ^ other) * part, part, axis=0)

    def project(held, other):
        matrix = jnp.concatenate([half_plane(j, other) for j in (2, 1, 3, 0)], axis=0)
        return jnp.dot(held, matrix, preferred_element_type=F32)

    projected = (project(far_held, 1) + project(near_held, 0)).astype(BF16)
    projected = projected.reshape(NY, rows, columns)
    ordered = []
    for row in range(NY):
        k = (row - y) % NY
        place = jnp.where(k == 0, 0, k % 3 + 1)
        ordered.append(lax.dynamic_slice_in_dim(projected, place, 1, axis=0))
    keys_values = jnp.concatenate(ordered, axis=0).reshape(cotangent.shape)

    pieces = after(pieces, keys_values)
    gradient = block(near, quarter)
    for piece in pieces:
        gradient = gradient + piece.astype(F32)

    gradient = gradient.reshape(first_moment.shape)
    first_next = 0.9 * first_moment + 0.1 * gradient
    second_next = 0.95 * second_moment + 0.05 * gradient * gradient
    weight_float = weights.astype(F32)
    update = first_next / (1.0 - 0.9**10) / (jnp.sqrt(second_next / (1.0 - 0.95**10)) + 1e-08)
    weights_next = (weight_float - 0.001 * (update + 0.1 * weight_float)).astype(BF16)

    local_float = frag_local[0].astype(F32)
    pair = (local_float + swap_replica(frag_local[0], 1).astype(F32)).astype(BF16)
    summed = pair.astype(F32) + swap_replica(after(pair, far), 2).astype(F32)
    outer_step = frag_global - summed / lax.axis_size("replica")
    moment_next = 0.9 * frag_moment + outer_step
    global_next = frag_global - 0.7 * (outer_step + 0.9 * moment_next)
    local_next = (0.5 * local_float + 0.5 * global_next).astype(BF16)[None]
    return (
        keys_values,
        weights_next,
        first_next,
        second_next,
        global_next,
        moment_next,
        local_next,
    )


def solution(mesh):
    return jax.shard_map(
        body,
        mesh=mesh,
        in_specs=(
            P(("replica", "fsdp", "tensor"), None),
            P(("replica", "fsdp"), None, "tensor"),
            P("replica", "fsdp", None, "tensor"),
            P("replica", "fsdp", None, "tensor"),
            P("replica", "fsdp", None, "tensor"),
            P("fsdp", None, "tensor"),
            P("fsdp", None, "tensor"),
            P("replica", "fsdp", None, "tensor"),
        ),
        out_specs=(
            P(("replica", "fsdp"), None, "tensor"),
            P("replica", "fsdp", None, "tensor"),
            P("replica", "fsdp", None, "tensor"),
            P("replica", "fsdp", None, "tensor"),
            P("fsdp", None, "tensor"),
            P("fsdp", None, "tensor"),
            P("replica", "fsdp", None, "tensor"),
        ),
        check_vma=False,
    )
```

```python
import jax
import jax.numpy as jnp
from jax import lax
from jax.sharding import PartitionSpec as P

NX, NZ, NY = 4, 8, 4
HALF = NZ // 2
BF16, F32 = jnp.bfloat16, jnp.float32


def move(value, target):
    pairs = []
    for x in range(NX):
        for z in range(NZ):
            to_x, to_z = target(x, z)
            pairs.append((NZ * x + z, NZ * (to_x % NX) + to_z))
    return lax.ppermute(value, "fsdp", pairs)


def move_x(value, shift):
    return move(value, lambda x, z: (x + shift, z))


def move_y(value, shift):
    return lax.ppermute(value, "tensor", [(y, (y + shift) % NY) for y in range(NY)])


def swap_z(value, bit):
    return move(value, lambda x, z: (x, z ^ bit))


def swap_replica(value, bit):
    return lax.ppermute(value, "replica", [(r, r ^ bit) for r in range(lax.axis_size("replica"))])


def after(value, *others):
    return lax.optimization_barrier((value, *others))[0]


def body(
    tokens, cotangent, weights, first_moment, second_moment, frag_global, frag_moment, frag_local
):
    rows, width = tokens.shape
    depth = weights.shape[1]
    columns = weights.shape[2] * weights.shape[3]
    part = HALF * depth
    x = lax.axis_index("fsdp") // NZ
    z = lax.axis_index("fsdp") % NZ
    side = z // HALF
    y = lax.axis_index("tensor")

    def lot(half):
        starts = [(x + j) % NX * (NZ * depth) + half * part for j in (2, 1, 3, 0)]
        return jnp.concatenate(
            [lax.dynamic_slice_in_dim(tokens, start, part, axis=1) for start in starts], axis=1
        )

    far_own, near_own = lot(1 - side), lot(side)

    own = after(weights[0], far_own).reshape(1, depth, columns)
    two = jnp.stack([own, swap_z(own, 4)])
    four = jnp.stack([two, swap_z(two, 2)])

    far_before, far_behind = move_y(far_own, 1), move_y(far_own, -1)
    far_before, far_behind, four = lax.optimization_barrier((far_before, far_behind, four))
    far_opposite = move_y(far_before, 1)
    near_own, far_behind = lax.optimization_barrier((near_own, far_behind))
    near_behind = move_y(near_own, -1)

    eight = jnp.stack([four, swap_z(four, 1)])
    eight = eight.reshape(2, 2, 2, depth, columns)
    near_behind, far_opposite, eight = lax.optimization_barrier((near_behind, far_opposite, eight))
    near_opposite = move_y(near_behind, -1)
    near_own, far_opposite = lax.optimization_barrier((near_own, far_opposite))
    near_before = move_y(near_own, 1)
    far_held = jnp.concatenate([far_own, far_before, far_behind, far_opposite], axis=0)
    near_held = jnp.concatenate([near_own, near_before, near_behind, near_opposite], axis=0)

    eight = jnp.where((z & 1) == 0, eight, eight[::-1])
    eight = jnp.where((z & 2) == 0, eight, eight[:, ::-1])
    eight = jnp.where((z & 4) == 0, eight, eight[:, :, ::-1])
    plane = eight.transpose(2, 1, 0, 3, 4).reshape(2 * part, columns)

    cot = cotangent.reshape(NY, rows, columns)
    cot = jnp.concatenate(
        [lax.dynamic_slice_in_dim(cot, (y + k) % NY, 1, axis=0) for k in (0, 3, 1, 2)], axis=0
    ).reshape(NY * rows, columns)

    def terms(held):
        product = lax.dot_general(held, cot, (((0,), (0,)), ((), ())), preferred_element_type=F32)
        return product.astype(BF16).reshape(NX, part, columns)

    def send_x(opposite, up, down, sign):
        if sign < 0:
            up, down = down, up
        passed = move_x(opposite, sign)
        reverse = move_x(down, -sign)
        return (up.astype(F32) + passed.astype(F32)).astype(BF16), reverse

    opposite, up, down, here = terms(far_held)
    up, reverse = send_x(opposite, up, down, 1)
    up, plane = lax.optimization_barrier((up, plane))
    forward = move_x(up, 1)
    far = here.astype(F32) + reverse.astype(F32) + forward.astype(F32)
    def halve(value, bit):
        value = value.reshape(-1, 2, depth, columns)
        low = (z & bit) == 0
        kept = jnp.where(low, value[:, 0], value[:, 1])
        given = jnp.where(low, value[:, 1], value[:, 0])
        return kept + swap_z(given.astype(BF16), bit).astype(F32)

    crossing = swap_z(halve(halve(far, 1), 2)[0].astype(BF16), 4).astype(F32)

    low = move_x(plane, 1)
    high = move_x(plane, -1)
    planes = {0: plane, 1: high, 2: move_x(low, 1), 3: low}

    opposite, up, down, here = terms(near_held)
    down, reverse = send_x(opposite, up, down, -1)
    forward = move_x(down, -1)
    near = here.astype(F32) + reverse.astype(F32) + forward.astype(F32)
    groups = [[NZ * i + HALF * h + k for k in range(HALF)] for i in range(NX) for h in range(2)]
    pieces = lax.all_to_all(
        near.astype(BF16).reshape(HALF, depth, columns), "fsdp", 0, 0, axis_index_groups=groups
    )

    def half_plane(j, other):
        return lax.dynamic_slice_in_dim(planes[j], (side ^ other) * part, part, axis=0)

    def project(held, other):
        matrix = jnp.concatenate([half_plane(j, other) for j in (2, 1, 3, 0)], axis=0)
        return jnp.dot(held, matrix, preferred_element_type=F32)

    projected = (project(far_held, 1) + project(near_held, 0)).astype(BF16)
    projected = projected.reshape(NY, rows, columns)
    ordered = []
    for row in range(NY):
        k = (row - y) % NY
        place = jnp.where(k == 0, 0, k % 3 + 1)
        ordered.append(lax.dynamic_slice_in_dim(projected, place, 1, axis=0))
    keys_values = jnp.concatenate(ordered, axis=0).reshape(cotangent.shape)

    gradient = pieces.astype(F32).sum(axis=0) + crossing

    gradient = gradient.reshape(first_moment.shape)
    first_next = 0.9 * first_moment + 0.1 * gradient
    second_next = 0.95 * second_moment + 0.05 * gradient * gradient
    weight_float = weights.astype(F32)
    update = first_next / (1.0 - 0.9**10) / (jnp.sqrt(second_next / (1.0 - 0.95**10)) + 1e-08)
    weights_next = (weight_float - 0.001 * (update + 0.1 * weight_float)).astype(BF16)

    local_float = frag_local[0].astype(F32)
    pair = (local_float + swap_replica(frag_local[0], 1).astype(F32)).astype(BF16)
    summed = pair.astype(F32) + swap_replica(after(pair, eight), 2).astype(F32)
    outer_step = frag_global - summed / lax.axis_size("replica")
    moment_next = 0.9 * frag_moment + outer_step
    global_next = frag_global - 0.7 * (outer_step + 0.9 * moment_next)
    local_next = (0.5 * local_float + 0.5 * global_next).astype(BF16)[None]
    return (
        keys_values,
        weights_next,
        first_next,
        second_next,
        global_next,
        moment_next,
        local_next,
    )


def solution(mesh):
    return jax.shard_map(
        body,
        mesh=mesh,
        in_specs=(
            P(("replica", "fsdp", "tensor"), None),
            P(("replica", "fsdp"), None, "tensor"),
            P("replica", "fsdp", None, "tensor"),
            P("replica", "fsdp", None, "tensor"),
            P("replica", "fsdp", None, "tensor"),
            P("fsdp", None, "tensor"),
            P("fsdp", None, "tensor"),
            P("replica", "fsdp", None, "tensor"),
        ),
        out_specs=(
            P(("replica", "fsdp"), None, "tensor"),
            P("replica", "fsdp", None, "tensor"),
            P("replica", "fsdp", None, "tensor"),
            P("replica", "fsdp", None, "tensor"),
            P("fsdp", None, "tensor"),
            P("fsdp", None, "tensor"),
            P("replica", "fsdp", None, "tensor"),
        ),
        check_vma=False,
    )
```

```python
import jax
import jax.numpy as jnp
from jax import lax
from jax.sharding import PartitionSpec as P

NX, NZ, NY = 4, 8, 4
HALF = NZ // 2
BF16, F32 = jnp.bfloat16, jnp.float32
ALONG_X = [[NZ * x + z for x in range(NX)] for z in range(NZ)]
IN_HALF = [[NZ * x + HALF * h + k for k in range(HALF)] for x in range(NX) for h in range(2)]


def move_y(value, shift):
    return lax.ppermute(value, "tensor", [(y, (y + shift) % NY) for y in range(NY)])


def swap_z(value, bit):
    pairs = [(NZ * x + z, NZ * x + (z ^ bit)) for x in range(NX) for z in range(NZ)]
    return lax.ppermute(value, "fsdp", pairs)


def exchange(value, groups):
    return lax.all_to_all(value, "fsdp", 0, 0, axis_index_groups=groups)


def move_x(value, shift):
    pairs = [(NZ * x + z, NZ * ((x + shift) % NX) + z) for x in range(NX) for z in range(NZ)]
    return lax.ppermute(value, "fsdp", pairs)


def swap_replica(value, bit):
    return lax.ppermute(value, "replica", [(r, r ^ bit) for r in range(lax.axis_size("replica"))])


def body(
    tokens, cotangent, weights, first_moment, second_moment, frag_global, frag_moment, frag_local
):
    rows = tokens.shape[0]
    depth = weights.shape[1]
    columns = weights.shape[2] * weights.shape[3]
    part = HALF * depth
    x = lax.axis_index("fsdp") // NZ
    z = lax.axis_index("fsdp") % NZ
    side = z // HALF
    y = lax.axis_index("tensor")

    def pick(value, index):
        return lax.dynamic_index_in_dim(value, index, axis=0, keepdims=False)

    def lot(half):
        starts = [i * NZ * depth + half * part for i in range(NX)]
        return jnp.concatenate(
            [lax.dynamic_slice_in_dim(tokens, start, part, axis=1) for start in starts], axis=1
        )

    far_own, near_own = lot(1 - side), lot(side)
    far_own, block, local = lax.optimization_barrier((far_own, weights[0], frag_local[0]))
    far_before, far_behind = move_y(far_own, 1), move_y(far_own, -1)

    def joined(value, bit, axis):
        moved = swap_z(value, bit)
        low = (z & bit) == 0
        pair = (jnp.where(low, value, moved), jnp.where(low, moved, value))
        return jnp.concatenate(pair, axis=axis)

    block = block.reshape(1, depth, columns)
    two = jnp.concatenate([block, swap_z(block, 4)])
    four = joined(two, 2, 1)

    core = lax.axis_index("replica") % 2
    halves = local.reshape(2, depth // 2, *local.shape[1:])
    mine, other = pick(halves, core), pick(halves, 1 - core)
    pair = (mine.astype(F32) + swap_replica(other, 1).astype(F32)).astype(BF16)
    total = pair.astype(F32) + swap_replica(pair, 2).astype(F32)

    far_before, far_behind, near_own, four, total = lax.optimization_barrier(
        (far_before, far_behind, near_own, four, total)
    )
    far_opposite = move_y(far_before, 1)
    near_behind = move_y(near_own, -1)
    eight = joined(four.reshape(2, 2, depth, columns), 1, 2).reshape(2, part, columns)
    near_behind, far_opposite, near_own, eight = lax.optimization_barrier(
        (near_behind, far_opposite, near_own, eight)
    )
    near_opposite = move_y(near_behind, -1)
    near_before = move_y(near_own, 1)
    far_held = (far_own, far_before, far_behind, far_opposite)
    low, high = move_x(eight, 1), move_x(eight, -1)
    planes = (eight, high, move_x(low, 1), low)
    cot = cotangent.reshape(NY, rows, columns)
    cot = jnp.concatenate(
        [lax.dynamic_slice_in_dim(cot, (y + k) % NY, 1, axis=0) for k in (0, 3, 1, 2)], axis=0
    ).reshape(NY * rows, columns)

    def terms(held):
        terms = lax.dot_general(held, cot, (((0,), (0,)), ((), ())), preferred_element_type=F32)
        return terms.astype(BF16).reshape(NX, part, columns)

    def halve(value, bit):
        value = value.reshape(-1, 2, depth, columns)
        low = (z & bit) == 0
        kept = jnp.where(low, value[:, 0], value[:, 1])
        given = jnp.where(low, value[:, 1], value[:, 0])
        return kept + swap_z(given.astype(BF16), bit).astype(F32)

    far = terms(jnp.concatenate(far_held, axis=0))
    far, total, near_own, near_behind, far_held = lax.optimization_barrier(
        (far, total, near_own, near_behind, far_held)
    )
    blank = jnp.zeros_like(near_own)
    near_rest = jnp.concatenate([near_own, blank, near_behind, blank], axis=0)
    far_held = jnp.concatenate(far_held, axis=0)
    far_held, near_rest = lax.optimization_barrier((far_held, near_rest))
    far = exchange(far, ALONG_X)
    far, near_before, near_opposite = lax.optimization_barrier((far, near_before, near_opposite))
    near_held = lax.dynamic_update_slice(near_rest, near_before, (rows, 0))
    near_held = lax.dynamic_update_slice(near_held, near_opposite, (3 * rows, 0))
    far = far.astype(F32).sum(axis=0)
    crossing = swap_z(halve(halve(far, 1), 2)[0].astype(BF16), 4)
    near = exchange(terms(near_held), ALONG_X).astype(F32).sum(axis=0).astype(BF16)
    near = exchange(near.reshape(HALF, depth, columns), IN_HALF)

    def matrix(other):
        halves = [plane[other] for plane in planes]
        return jnp.concatenate([lax.select_n((i - x) % NX, *halves) for i in range(NX)], axis=0)

    far_matrix, near_matrix = lax.optimization_barrier((matrix(1), matrix(0)))
    projected = jnp.dot(far_held, far_matrix, preferred_element_type=F32)
    projected = projected + jnp.dot(near_held, near_matrix, preferred_element_type=F32)
    projected = projected.astype(BF16).reshape(NY, rows, columns)
    ordered = []
    for row in range(NY):
        k = (row - y) % NY
        place = jnp.where(k == 0, 0, k % 3 + 1)
        ordered.append(lax.dynamic_slice_in_dim(projected, place, 1, axis=0))
    keys_values = jnp.concatenate(ordered, axis=0).reshape(cotangent.shape)

    near, keys_values = lax.optimization_barrier((near, keys_values))
    gradient = near.astype(F32).sum(axis=0) + crossing.astype(F32)
    gradient = gradient.reshape(first_moment.shape)
    first_next = 0.9 * first_moment + 0.1 * gradient
    second_next = 0.95 * second_moment + 0.05 * gradient * gradient
    weight_float = weights.astype(F32)
    update = first_next / (1.0 - 0.9**10) / (jnp.sqrt(second_next / (1.0 - 0.95**10)) + 1e-08)
    weights_next = (weight_float - 0.001 * (update + 0.1 * weight_float)).astype(BF16)

    local_float = frag_local[0].astype(F32)
    total = jnp.stack([total, swap_replica(total, 1)])
    summed = jnp.where(core == 0, total, total[::-1]).reshape(frag_global.shape)
    outer_step = frag_global - summed / lax.axis_size("replica")
    moment_next = 0.9 * frag_moment + outer_step
    global_next = frag_global - 0.7 * (outer_step + 0.9 * moment_next)
    local_next = (0.5 * local_float + 0.5 * global_next).astype(BF16)[None]
    return (
        keys_values,
        weights_next,
        first_next,
        second_next,
        global_next,
        moment_next,
        local_next,
    )


def solution(mesh):
    return jax.shard_map(
        body,
        mesh=mesh,
        in_specs=(
            P(("replica", "fsdp", "tensor"), None),
            P(("replica", "fsdp"), None, "tensor"),
            P("replica", "fsdp", None, "tensor"),
            P("replica", "fsdp", None, "tensor"),
            P("replica", "fsdp", None, "tensor"),
            P("fsdp", None, "tensor"),
            P("fsdp", None, "tensor"),
            P("replica", "fsdp", None, "tensor"),
        ),
        out_specs=(
            P(("replica", "fsdp"), None, "tensor"),
            P("replica", "fsdp", None, "tensor"),
            P("replica", "fsdp", None, "tensor"),
            P("replica", "fsdp", None, "tensor"),
            P("fsdp", None, "tensor"),
            P("fsdp", None, "tensor"),
            P("replica", "fsdp", None, "tensor"),
        ),
        check_vma=False,
    )
```

```python
import jax
import jax.numpy as jnp
from jax import lax
from jax.sharding import PartitionSpec as P

NX, NZ, NY = 4, 8, 4
HALF = NZ // 2
BF16, F32 = jnp.bfloat16, jnp.float32


def move(value, target):
    pairs = []
    for x in range(NX):
        for z in range(NZ):
            to_x, to_z = target(x, z)
            pairs.append((NZ * x + z, NZ * (to_x % NX) + to_z))
    return lax.ppermute(value, "fsdp", pairs)


def move_x(value, shift):
    return move(value, lambda x, z: (x + shift, z))


def move_y(value, shift):
    return lax.ppermute(value, "tensor", [(y, (y + shift) % NY) for y in range(NY)])


def swap_z(value, bit):
    return move(value, lambda x, z: (x, z ^ bit))


def swap_replica(value, bit):
    return lax.ppermute(value, "replica", [(r, r ^ bit) for r in range(lax.axis_size("replica"))])


def after(value, *others):
    return lax.optimization_barrier((value, *others))[0]


def body(
    tokens, cotangent, weights, first_moment, second_moment, frag_global, frag_moment, frag_local
):
    rows, width = tokens.shape
    depth = weights.shape[1]
    columns = weights.shape[2] * weights.shape[3]
    part = HALF * depth
    x = lax.axis_index("fsdp") // NZ
    z = lax.axis_index("fsdp") % NZ
    side = z // HALF
    y = lax.axis_index("tensor")

    def lot(half):
        starts = [(x + j) % NX * (NZ * depth) + half * part for j in (2, 1, 3, 0)]
        return jnp.concatenate(
            [lax.dynamic_slice_in_dim(tokens, start, part, axis=1) for start in starts], axis=1
        )

    far_own, near_own = lot(1 - side), lot(side)

    own = after(weights[0], far_own).reshape(1, depth, columns)
    two = jnp.stack([own, swap_z(own, 4)])
    four = jnp.stack([two, swap_z(two, 2)])

    far_before, far_behind = move_y(far_own, 1), move_y(far_own, -1)
    far_before, far_behind, four = lax.optimization_barrier((far_before, far_behind, four))
    far_opposite = move_y(far_before, 1)
    near_own, far_behind = lax.optimization_barrier((near_own, far_behind))
    near_behind = move_y(near_own, -1)

    eight = jnp.stack([four, swap_z(four, 1)])
    eight = eight.reshape(2, 2, 2, depth, columns)
    near_behind, far_opposite, eight = lax.optimization_barrier((near_behind, far_opposite, eight))
    near_opposite = move_y(near_behind, -1)
    near_own, far_opposite = lax.optimization_barrier((near_own, far_opposite))
    near_before = move_y(near_own, 1)
    far_held = jnp.concatenate([far_own, far_before, far_behind, far_opposite], axis=0)
    near_held = jnp.concatenate([near_own, near_before, near_behind, near_opposite], axis=0)

    eight = jnp.where((z & 1) == 0, eight, eight[::-1])
    eight = jnp.where((z & 2) == 0, eight, eight[:, ::-1])
    eight = jnp.where((z & 4) == 0, eight, eight[:, :, ::-1])
    plane = eight.transpose(2, 1, 0, 3, 4).reshape(2 * part, columns)

    cot = cotangent.reshape(NY, rows, columns)
    cot = jnp.concatenate(
        [lax.dynamic_slice_in_dim(cot, (y + k) % NY, 1, axis=0) for k in (0, 3, 1, 2)], axis=0
    ).reshape(NY * rows, columns)

    def terms(held):
        product = lax.dot_general(held, cot, (((0,), (0,)), ((), ())), preferred_element_type=F32)
        return product.astype(BF16).reshape(NX, part, columns)

    def send_x(opposite, up, down, sign):
        if sign < 0:
            up, down = down, up
        passed = move_x(opposite, sign)
        reverse = move_x(down, -sign)
        return (up.astype(F32) + passed.astype(F32)).astype(BF16), reverse

    opposite, up, down, here = terms(far_held)
    up, reverse = send_x(opposite, up, down, 1)
    far_rows = lax.optimization_barrier(far_held)
    up, plane, far_rows = lax.optimization_barrier((up, plane, far_rows))
    forward = move_x(up, 1)
    far = here.astype(F32) + reverse.astype(F32) + forward.astype(F32)
    def halve(value, bit):
        value = value.reshape(-1, 2, depth, columns)
        low = (z & bit) == 0
        kept = jnp.where(low, value[:, 0], value[:, 1])
        given = jnp.where(low, value[:, 1], value[:, 0])
        return kept + swap_z(given.astype(BF16), bit).astype(F32)

    crossing = swap_z(halve(halve(far, 1), 2)[0].astype(BF16), 4).astype(F32)

    low = move_x(plane, 1)
    high = move_x(plane, -1)
    planes = {0: plane, 1: high, 2: move_x(low, 1), 3: low}

    opposite, up, down, here = terms(near_held)
    down, reverse = send_x(opposite, up, down, -1)
    near_rows = lax.optimization_barrier(near_held)
    down, near_rows = lax.optimization_barrier((down, near_rows))
    forward = move_x(down, -1)
    near = here.astype(F32) + reverse.astype(F32) + forward.astype(F32)
    groups = [[NZ * i + HALF * h + k for k in range(HALF)] for i in range(NX) for h in range(2)]
    pieces = lax.all_to_all(
        near.astype(BF16).reshape(HALF, depth, columns), "fsdp", 0, 0, axis_index_groups=groups
    )

    def half_plane(j, other):
        return lax.dynamic_slice_in_dim(planes[j], (side ^ other) * part, part, axis=0)

    def matrix(other):
        return jnp.concatenate([half_plane(j, other) for j in (2, 1, 3, 0)], axis=0)

    far_matrix, near_matrix = lax.optimization_barrier((matrix(1), matrix(0)))
    projected = jnp.dot(far_rows, far_matrix, preferred_element_type=F32)
    projected = projected + jnp.dot(near_rows, near_matrix, preferred_element_type=F32)
    projected = projected.astype(BF16)
    projected = projected.reshape(NY, rows, columns)
    ordered = []
    for row in range(NY):
        k = (row - y) % NY
        place = jnp.where(k == 0, 0, k % 3 + 1)
        ordered.append(lax.dynamic_slice_in_dim(projected, place, 1, axis=0))
    keys_values = jnp.concatenate(ordered, axis=0).reshape(cotangent.shape)

    pieces, keys_values = lax.optimization_barrier((pieces, keys_values))
    gradient = pieces.astype(F32).sum(axis=0) + crossing

    gradient = gradient.reshape(first_moment.shape)
    first_next = 0.9 * first_moment + 0.1 * gradient
    second_next = 0.95 * second_moment + 0.05 * gradient * gradient
    weight_float = weights.astype(F32)
    update = first_next / (1.0 - 0.9**10) / (jnp.sqrt(second_next / (1.0 - 0.95**10)) + 1e-08)
    weights_next = (weight_float - 0.001 * (update + 0.1 * weight_float)).astype(BF16)

    local_float = frag_local[0].astype(F32)
    pair = (local_float + swap_replica(frag_local[0], 1).astype(F32)).astype(BF16)
    summed = pair.astype(F32) + swap_replica(after(pair, eight), 2).astype(F32)
    outer_step = frag_global - summed / lax.axis_size("replica")
    moment_next = 0.9 * frag_moment + outer_step
    global_next = frag_global - 0.7 * (outer_step + 0.9 * moment_next)
    local_next = (0.5 * local_float + 0.5 * global_next).astype(BF16)[None]
    return (
        keys_values,
        weights_next,
        first_next,
        second_next,
        global_next,
        moment_next,
        local_next,
    )


def solution(mesh):
    return jax.shard_map(
        body,
        mesh=mesh,
        in_specs=(
            P(("replica", "fsdp", "tensor"), None),
            P(("replica", "fsdp"), None, "tensor"),
            P("replica", "fsdp", None, "tensor"),
            P("replica", "fsdp", None, "tensor"),
            P("replica", "fsdp", None, "tensor"),
            P("fsdp", None, "tensor"),
            P("fsdp", None, "tensor"),
            P("replica", "fsdp", None, "tensor"),
        ),
        out_specs=(
            P(("replica", "fsdp"), None, "tensor"),
            P("replica", "fsdp", None, "tensor"),
            P("replica", "fsdp", None, "tensor"),
            P("replica", "fsdp", None, "tensor"),
            P("fsdp", None, "tensor"),
            P("fsdp", None, "tensor"),
            P("replica", "fsdp", None, "tensor"),
        ),
        check_vma=False,
    )
```

```python
import jax
import jax.numpy as jnp
from jax import lax
from jax.sharding import PartitionSpec as P

NX, NZ, NY = 4, 8, 4
HALF = NZ // 2
BF16, F32 = jnp.bfloat16, jnp.float32


def move(value, target):
    pairs = []
    for x in range(NX):
        for z in range(NZ):
            to_x, to_z = target(x, z)
            pairs.append((NZ * x + z, NZ * (to_x % NX) + to_z))
    return lax.ppermute(value, "fsdp", pairs)


def move_x(value, shift):
    return move(value, lambda x, z: (x + shift, z))


def move_y(value, shift):
    return lax.ppermute(value, "tensor", [(y, (y + shift) % NY) for y in range(NY)])


def swap_z(value, bit):
    return move(value, lambda x, z: (x, z ^ bit))


def swap_replica(value, bit):
    return lax.ppermute(value, "replica", [(r, r ^ bit) for r in range(lax.axis_size("replica"))])


def after(value, *others):
    return lax.optimization_barrier((value, *others))[0]


def body(
    tokens, cotangent, weights, first_moment, second_moment, frag_global, frag_moment, frag_local
):
    rows, width = tokens.shape
    depth = weights.shape[1]
    columns = weights.shape[2] * weights.shape[3]
    part = HALF * depth
    x = lax.axis_index("fsdp") // NZ
    z = lax.axis_index("fsdp") % NZ
    side = z // HALF
    y = lax.axis_index("tensor")

    def lot(half):
        starts = [(x + j) % NX * (NZ * depth) + half * part for j in (2, 1, 3, 0)]
        return jnp.concatenate(
            [lax.dynamic_slice_in_dim(tokens, start, part, axis=1) for start in starts], axis=1
        )

    far_own, near_own = lot(1 - side), lot(side)

    own = after(weights[0], far_own).reshape(1, depth, columns)
    two = jnp.stack([own, swap_z(own, 4)])
    four = jnp.stack([two, swap_z(two, 2)])

    far_before, far_behind = move_y(far_own, 1), move_y(far_own, -1)
    far_before, far_behind, four = lax.optimization_barrier((far_before, far_behind, four))
    far_opposite = move_y(far_before, 1)
    near_own, far_behind = lax.optimization_barrier((near_own, far_behind))
    near_behind = move_y(near_own, -1)

    eight = jnp.stack([four, swap_z(four, 1)])
    eight = eight.reshape(2, 2, 2, depth, columns)
    near_behind, far_opposite, eight = lax.optimization_barrier((near_behind, far_opposite, eight))
    near_opposite = move_y(near_behind, -1)
    near_own, far_opposite = lax.optimization_barrier((near_own, far_opposite))
    near_before = move_y(near_own, 1)
    far_held = jnp.concatenate([far_own, far_before, far_behind, far_opposite], axis=0)
    near_held = jnp.concatenate([near_own, near_before, near_behind, near_opposite], axis=0)

    eight = jnp.where((z & 1) == 0, eight, eight[::-1])
    eight = jnp.where((z & 2) == 0, eight, eight[:, ::-1])
    eight = jnp.where((z & 4) == 0, eight, eight[:, :, ::-1])
    plane = eight.transpose(2, 1, 0, 3, 4).reshape(2 * part, columns)

    cot = cotangent.reshape(NY, rows, columns)
    cot = jnp.concatenate(
        [lax.dynamic_slice_in_dim(cot, (y + k) % NY, 1, axis=0) for k in (0, 3, 1, 2)], axis=0
    ).reshape(NY * rows, columns)

    def terms(held):
        product = lax.dot_general(held, cot, (((0,), (0,)), ((), ())), preferred_element_type=F32)
        return product.astype(BF16).reshape(NX, part, columns)

    def send_x(opposite, up, down, sign):
        if sign < 0:
            up, down = down, up
        passed = move_x(opposite, sign)
        reverse = move_x(down, -sign)
        return (up.astype(F32) + passed.astype(F32)).astype(BF16), reverse

    opposite, up, down, here = terms(far_held)
    up, reverse = send_x(opposite, up, down, 1)
    far_rows = lax.optimization_barrier(far_held)
    up, far_rows = lax.optimization_barrier((up, far_rows))
    forward = move_x(up, 1)
    far = here.astype(F32) + reverse.astype(F32) + forward.astype(F32)
    def halve(value, bit):
        value = value.reshape(-1, 2, depth, columns)
        low = (z & bit) == 0
        kept = jnp.where(low, value[:, 0], value[:, 1])
        given = jnp.where(low, value[:, 1], value[:, 0])
        return kept + swap_z(given.astype(BF16), bit).astype(F32)

    crossing = swap_z(halve(halve(far, 1), 2)[0].astype(BF16), 4).astype(F32)

    low = move_x(plane, 1)
    high = move_x(plane, -1)
    planes = {0: plane, 1: high, 2: move_x(low, 1), 3: low}

    opposite, up, down, here = terms(near_held)
    down, reverse = send_x(opposite, up, down, -1)
    near_rows = lax.optimization_barrier(near_held)
    down, near_rows = lax.optimization_barrier((down, near_rows))
    forward = move_x(down, -1)
    near = here.astype(F32) + reverse.astype(F32) + forward.astype(F32)
    groups = [[NZ * i + HALF * h + k for k in range(HALF)] for i in range(NX) for h in range(2)]
    pieces = lax.all_to_all(
        near.astype(BF16).reshape(HALF, depth, columns), "fsdp", 0, 0, axis_index_groups=groups
    )

    def half_plane(j, other):
        return lax.dynamic_slice_in_dim(planes[j], (side ^ other) * part, part, axis=0)

    def matrix(other):
        return jnp.concatenate([half_plane(j, other) for j in (2, 1, 3, 0)], axis=0)

    far_matrix, near_matrix = lax.optimization_barrier((matrix(1), matrix(0)))
    projected = jnp.dot(far_rows, far_matrix, preferred_element_type=F32)
    projected = projected + jnp.dot(near_rows, near_matrix, preferred_element_type=F32)
    projected = projected.astype(BF16)
    projected = projected.reshape(NY, rows, columns)
    ordered = []
    for row in range(NY):
        k = (row - y) % NY
        place = jnp.where(k == 0, 0, k % 3 + 1)
        ordered.append(lax.dynamic_slice_in_dim(projected, place, 1, axis=0))
    keys_values = jnp.concatenate(ordered, axis=0).reshape(cotangent.shape)

    pieces, keys_values = lax.optimization_barrier((pieces, keys_values))
    gradient = pieces.astype(F32).sum(axis=0) + crossing

    gradient = gradient.reshape(first_moment.shape)
    first_next = 0.9 * first_moment + 0.1 * gradient
    second_next = 0.95 * second_moment + 0.05 * gradient * gradient
    weight_float = weights.astype(F32)
    update = first_next / (1.0 - 0.9**10) / (jnp.sqrt(second_next / (1.0 - 0.95**10)) + 1e-08)
    weights_next = (weight_float - 0.001 * (update + 0.1 * weight_float)).astype(BF16)

    local_float = frag_local[0].astype(F32)
    pair = (local_float + swap_replica(frag_local[0], 1).astype(F32)).astype(BF16)
    pair = after(pair, up)
    summed = pair.astype(F32) + swap_replica(pair, 2).astype(F32)
    outer_step = frag_global - summed / lax.axis_size("replica")
    moment_next = 0.9 * frag_moment + outer_step
    global_next = frag_global - 0.7 * (outer_step + 0.9 * moment_next)
    local_next = (0.5 * local_float + 0.5 * global_next).astype(BF16)[None]
    return (
        keys_values,
        weights_next,
        first_next,
        second_next,
        global_next,
        moment_next,
        local_next,
    )


def solution(mesh):
    return jax.shard_map(
        body,
        mesh=mesh,
        in_specs=(
            P(("replica", "fsdp", "tensor"), None),
            P(("replica", "fsdp"), None, "tensor"),
            P("replica", "fsdp", None, "tensor"),
            P("replica", "fsdp", None, "tensor"),
            P("replica", "fsdp", None, "tensor"),
            P("fsdp", None, "tensor"),
            P("fsdp", None, "tensor"),
            P("replica", "fsdp", None, "tensor"),
        ),
        out_specs=(
            P(("replica", "fsdp"), None, "tensor"),
            P("replica", "fsdp", None, "tensor"),
            P("replica", "fsdp", None, "tensor"),
            P("replica", "fsdp", None, "tensor"),
            P("fsdp", None, "tensor"),
            P("fsdp", None, "tensor"),
            P("replica", "fsdp", None, "tensor"),
        ),
        check_vma=False,
    )
```
